32 devices in a mesh: rep: 8 (over y, x, core), ep: 4 (over z).
Axes of the slice: x: 2, y: 2, z: 4, core: 2. Of those that a mesh axis runs over, the one named last changes fastest.
Arguments:
- tokens: bfloat16 [4096, 2048], P(('rep', 'ep')), may hold values from -6 to 6
- experts: int32 [4096, 2], P(('rep', 'ep')), may hold values from 0 to 3, all different within a row; in each aligned block of 128 rows (0 to 127, 128 to 255, ...) at most 96 rows name the same one
- gates: bfloat16 [4096, 2], P(('rep', 'ep')), may hold values from 0.099609375 to 1
- w_gate: bfloat16 [4, 2048, 1408], P('ep'), may hold values from -0.125 to 0.125
- w_up: bfloat16 [4, 2048, 1408], P('ep'), may hold values from -0.125 to 0.125
- w_down: bfloat16 [4, 1408, 2048], P('ep'), may hold values from -0.15625 to 0.15625
- cotangent: bfloat16 [4096, 2048], P(('rep', 'ep')), may hold values from -1.1953125 to 1.1953125
Outputs:
- layer_out: bfloat16 [4096, 2048], P(('rep', 'ep'))
- input_grads: bfloat16 [4096, 2048], P(('rep', 'ep'))
- gate_grads: bfloat16 [4096, 2], P(('rep', 'ep'))
- grad_gate: float32 [4, 2048, 1408], P('ep', 'rep')
- grad_up: float32 [4, 2048, 1408], P('ep', 'rep')
- grad_down: float32 [4, 1408, 2048], P('ep', 'rep')
The draws below stay inside these ranges and needn't reach their ends.
Inputs may be any that keep to these rules, and one draw needn't show every extreme that they name: Each row names 2 different experts; the rows of one device name no expert more than 96 times, a bound that some block reaches.
All inputs are finite; a program needn't handle non-finite values.
Results may differ from the reference program's by a relative error of at most 0.013.
Values may be sent and summed in bfloat16 or wider, within the bound.
A program may use at most 128 MiB of HBM per device.

```python
import math
import jax
import jax.numpy as jnp
import numpy as np
from jax import lax

D = 2048
FF = 1408
TOP = 2
TOK_DEV = 128
EXPERTS = 4
CAP = 96
TOKENS = 4096
N_REP = 8
N_EP = 4


def spiked(result, key, source, target, blocks, factor):
    owner, partner = [(jnp.arange(result.shape[axis_at]) // (result.shape[axis_at] // blocks)).reshape([-1 if axis == axis_at else 1 for axis in range(result.ndim)]) for axis_at in (source, target)]
    chosen = jax.random.permutation(key, blocks)[partner]
    strong = (owner == chosen) | (owner == (partner + blocks // 2) % blocks)
    return jnp.where(strong, factor * result, result)


def block_scale(key, extent, shards, least, top_value):
    loudness = 1.0
    for axis_at, parts in shards:
        heights = jax.random.uniform(jax.random.fold_in(jax.random.fold_in(key, 6), axis_at), (parts,), jnp.float32, least / len(shards), top_value / len(shards))
        loudness = loudness * jnp.repeat(jnp.exp(heights), extent[axis_at] // parts).reshape((-1,) + (1,) * (len(extent) - 1 - axis_at))
    return loudness


def assign_block(stream_key, own, number, rows, number_of, top, reach, lean):
    order = jax.random.permutation(stream_key, number_of)
    crowded, common = shares(number_of, rows * top, reach, lean, True), shares(number_of, rows * top, reach, lean, False)
    places = jnp.arange(number_of)

    def named(tallies, rotation):
        used = int((tallies > 0).sum())
        fixed = max(1, used // 4)
        passed = fixed + (places - fixed + rotation * (used - fixed)) % max(1, number_of - fixed)
        return jnp.zeros((number_of,), jnp.int32).at[order[jnp.where(places < fixed, places, passed)]].set(jnp.asarray(tallies, jnp.int32))

    tallies = jnp.where(number % 4 == 0, named(crowded, number // 4), named(common, number - number // 4 - 1))
    mixed = jax.random.permutation(jax.random.fold_in(own, 3), number_of)
    donor, receiver = mixed[0:number_of // 2 * 2:2], mixed[1:number_of // 2 * 2:2]
    slack = jnp.minimum(tallies[donor] - 1, reach - tallies[receiver]) // 2
    slack = jnp.where((donor == order[0]) | (receiver == order[0]) | (tallies[receiver] == 0), 0, jnp.maximum(slack, 0))
    passed = jax.random.randint(jax.random.fold_in(own, 4), (number_of // 2,), 0, 1 << 20) % (slack + 1)
    tallies = tallies.at[donor].add(-passed).at[receiver].add(passed)
    items = jnp.searchsorted(jnp.cumsum(tallies), jnp.arange(rows * top), side="right").astype(jnp.int32)
    table = items.reshape(top, rows).T
    table = table[jax.random.permutation(jax.random.fold_in(own, 1), rows)]
    rotation = jax.random.randint(jax.random.fold_in(own, 2), (rows, 1), 0, top)
    return jnp.take_along_axis(table, (jnp.arange(top)[None, :] + rotation) % top, axis=1)


def shares(amount, total, bound, slope, full):
    portions = [(1 << 20) // math.isqrt(grade ** slope) + 1 for grade in range(1, amount + 1)]
    largest = bound if full else min(bound, max(-(-total // amount), total * portions[0] // sum(portions)))
    least = 1 if total - largest >= amount - 1 else 0
    given, rest = [largest] + [least] * (amount - 1), total - largest - least * (amount - 1)
    while rest > 0:
        candidates = [i for i in range(1, amount) if given[i] < largest] or [i for i in range(1, amount) if given[i] < bound]
        pool, budget = sum([portions[i] for i in candidates]), rest
        for i in candidates:
            extra = min(bound - given[i], max(1, budget * portions[i] // pool), rest)
            given[i] = given[i] + extra
            rest = rest - extra
    return np.array(given)


def bell_draw(stream_key, dims, scale, limit, split=(), held_as=jnp.bfloat16):
    values = scale * jax.random.normal(stream_key, dims, jnp.float32)
    if split:
        values = values * block_scale(stream_key, dims, split, -0.22, 0.18)
    return jnp.clip(values, -limit, limit).astype(held_as)


def heavy_noise(stream_key, extent, deviation, reach, shards, heavy, kind=jnp.bfloat16):
    entries = deviation * jax.random.normal(stream_key, extent, jnp.float32)
    if shards:
        entries = entries * block_scale(stream_key, extent, shards, -0.22, 0.18)
    return jnp.clip(spiked(entries, jax.random.fold_in(stream_key, 3), *heavy), -reach, reach).astype(kind)


def setup_inputs(seed: int = 0) -> dict:
    streams_of = jax.random.split(jax.random.key(seed), 8)
    tokens = heavy_noise(streams_of[0], (TOKENS, D), 1.0, 6.0, ((0, 32),), (0, 1, 32, 2.75))
    experts_keys = jax.random.split(jax.random.fold_in(streams_of[1], 1), TOKENS // TOK_DEV)
    experts_turns = jax.random.permutation(jax.random.fold_in(streams_of[1], 3), TOKENS // TOK_DEV)
    experts = jax.vmap(lambda own, number: assign_block(jax.random.fold_in(streams_of[1], 2), own, number, TOK_DEV, EXPERTS, TOP, CAP, 2))(experts_keys, experts_turns).reshape((TOKENS, TOP))
    gates = jnp.clip(jnp.exp(math.log(1.0) - 2.306499 * jax.random.uniform(streams_of[2], (TOKENS, TOP), jnp.float32) ** block_scale(streams_of[2], (TOKENS, TOP), ((0, 32),), -0.2, 0.2)), 0.099609375, 1.0).astype(jnp.bfloat16)
    w_gate = bell_draw(streams_of[3], (EXPERTS, D, FF), D ** -0.5, 0.125, ((0, 4),))
    w_up = bell_draw(streams_of[4], (EXPERTS, D, FF), D ** -0.5, 0.125, ((0, 4),))
    w_down = bell_draw(streams_of[5], (EXPERTS, FF, D), FF ** -0.5, 0.15625, ((0, 4),))
    cotangent = bell_draw(streams_of[6], (TOKENS, D), 0.2, 1.1953125, ((0, 32),))
    return {"tokens": tokens, "experts": experts, "gates": gates, "w_gate": w_gate, "w_up": w_up, "w_down": w_down, "cotangent": cotangent}


def store_bf16(value):
    return lax.optimization_barrier(value.astype(jnp.bfloat16)).astype(jnp.float32)


def reference(tokens, experts, gates, w_gate, w_up, w_down, cotangent):
    pair_count = TOK_DEV * TOP
    blocks = TOKENS // TOK_DEV
    flat_exp = experts.reshape(blocks, pair_count)
    onehot = (flat_exp[:, :, None] == jnp.arange(EXPERTS, dtype=jnp.int32)[None, None, :]).astype(jnp.int32)
    slot_rank = jnp.sum((jnp.cumsum(onehot, axis=1) - onehot) * onehot, axis=2)
    slot_index = (flat_exp * CAP + slot_rank).astype(jnp.int32)
    block_ids = jnp.broadcast_to(jnp.arange(blocks, dtype=jnp.int32)[:, None], (blocks, pair_count))
    global_pair = jnp.broadcast_to(jnp.arange(pair_count, dtype=jnp.int32)[None, :], (blocks, pair_count)) + block_ids * pair_count
    table = jnp.zeros((blocks, EXPERTS * CAP), jnp.int32).at[block_ids, slot_index].set(global_pair)
    filled = jnp.zeros((blocks, EXPERTS * CAP), jnp.float32).at[block_ids, slot_index].set(1.0)
    table = table.reshape(N_REP, N_EP, EXPERTS, CAP)
    filled = filled.reshape(N_REP, N_EP, EXPERTS, CAP)
    gate_flat = gates.reshape(-1).astype(jnp.float32)

    def expert_step(carry, expert_id):
        gate_mat = w_gate[expert_id].astype(jnp.float32)
        up_mat = w_up[expert_id].astype(jnp.float32)
        down_mat = w_down[expert_id].astype(jnp.float32)

        def group_step(inner, replica):
            out_acc, grad_acc, dots_acc, sum_gate, sum_up, sum_down = inner
            pair_ids = table[replica, :, expert_id, :].reshape(-1)
            live_rows = filled[replica, :, expert_id, :].reshape(-1)
            token_ids = pair_ids // TOP
            expert_in = tokens[token_ids].astype(jnp.float32) * live_rows[:, None]
            gate_pre = jnp.dot(expert_in, gate_mat)
            up_pre = jnp.dot(expert_in, up_mat)
            sigmoid_g = jax.nn.sigmoid(gate_pre)
            activated = gate_pre * sigmoid_g
            hidden = store_bf16(activated * up_pre)
            expert_out = store_bf16(jnp.dot(hidden, down_mat))
            weight_rows = gate_flat[pair_ids] * live_rows
            out_acc = out_acc.at[token_ids].add(weight_rows[:, None] * expert_out)
            cot_rows = cotangent[token_ids].astype(jnp.float32) * live_rows[:, None]
            dots_acc = dots_acc.at[pair_ids].add(live_rows * jnp.sum(cot_rows * expert_out, axis=1))
            scaled_grad = store_bf16(weight_rows[:, None] * cot_rows)
            hidden_grad = jnp.dot(scaled_grad, down_mat.T)
            gate_delta = store_bf16(hidden_grad * up_pre * sigmoid_g * (1.0 + gate_pre * (1.0 - sigmoid_g)))
            up_delta = store_bf16(hidden_grad * activated)
            row_grads = store_bf16(jnp.dot(gate_delta, gate_mat.T) + jnp.dot(up_delta, up_mat.T))
            grad_acc = grad_acc.at[token_ids].add(row_grads)
            sum_gate = sum_gate + store_bf16(jnp.dot(expert_in.T, gate_delta))
            sum_up = sum_up + store_bf16(jnp.dot(expert_in.T, up_delta))
            sum_down = sum_down + store_bf16(jnp.dot(hidden.T, scaled_grad))
            return (out_acc, grad_acc, dots_acc, sum_gate, sum_up, sum_down), None

        out_acc, grad_acc, dots_acc = carry
        zero_df = jnp.zeros((D, FF), jnp.float32)
        zero_fd = jnp.zeros((FF, D), jnp.float32)
        inner, unused = lax.scan(group_step, (out_acc, grad_acc, dots_acc, zero_df, zero_df, zero_fd), jnp.arange(N_REP, dtype=jnp.int32))
        return (inner[0], inner[1], inner[2]), (inner[3], inner[4], inner[5])

    start = (jnp.zeros((TOKENS, D), jnp.float32), jnp.zeros((TOKENS, D), jnp.float32), jnp.zeros((TOKENS * TOP,), jnp.float32))
    final, stacked = lax.scan(expert_step, start, jnp.arange(EXPERTS, dtype=jnp.int32))
    layer_out = final[0].astype(jnp.bfloat16)
    input_grads = final[1].astype(jnp.bfloat16)
    gate_grads = final[2].reshape(TOKENS, TOP).astype(jnp.bfloat16)
    return (layer_out, input_grads, gate_grads, stacked[0], stacked[1], stacked[2])
```

```python
import jax
import jax.numpy as jnp
from jax import lax
from jax.sharding import PartitionSpec as P

F32 = jnp.float32
BF16 = jnp.bfloat16


def dot(lhs, rhs, lhs_dim, rhs_dim):
    contract = (((lhs_dim,), (rhs_dim,)), ((), ()))
    return lax.dot_general(lhs, rhs, contract, preferred_element_type=F32)


def exchange(rows):
    return lax.all_to_all(rows, "ep", split_axis=0, concat_axis=0, tiled=True)


def after(value, *others):
    return lax.optimization_barrier((value, *others))[0]


def body(tokens, experts, gates, w_gate, w_up, w_down, cotangent):
    tok_rows, width = tokens.shape
    top_count = experts.shape[1]
    n_experts = lax.axis_size("ep")
    capacity = 3 * tok_rows * top_count // (2 * n_experts)
    slots = n_experts * capacity
    gate_mat, up_mat, down_mat = (w_gate[0], w_up[0], w_down[0])

    ids = jnp.arange(n_experts, dtype=jnp.int32)
    named = (experts[:, :, None] == ids).astype(BF16)
    visits = jnp.sum(named, axis=1)
    rows = jnp.arange(tok_rows, dtype=jnp.int32)
    earlier = (rows[:, None] > rows[None, :]).astype(BF16)
    rank = dot(earlier, visits, 1, 0)
    place = rank + (ids * capacity).astype(F32)[None, :]
    slot = jnp.sum(named.astype(F32) * place[:, None, :], axis=2).astype(jnp.int32)
    hit = [
        slot[:, k][:, None] == jnp.arange(slots, dtype=jnp.int32)[None, :]
        for k in range(top_count)
    ]
    picks = [h.astype(BF16) for h in hit]
    pick = sum(picks[1:], picks[0])
    weights = gates.astype(F32)

    dispatch = dot(pick, tokens, 0, 0).astype(BF16)
    rows_in = exchange(dispatch.reshape(n_experts, capacity, width)).reshape(slots, width)

    slot_gate = sum(
        jnp.sum(h.astype(F32) * weights[:, k][:, None], axis=0) for k, h in enumerate(hit)
    )
    grad_disp = (dot(pick, cotangent, 0, 0) * slot_gate[:, None]).astype(BF16)
    out_grads = exchange(
        after(grad_disp, rows_in).reshape(n_experts, capacity, width)
    ).reshape(slots, width)

    gate_pre = dot(rows_in, gate_mat, 1, 0)
    up_pre = dot(rows_in, up_mat, 1, 0)
    sigmoid_g = jax.nn.sigmoid(gate_pre)
    activated = gate_pre * sigmoid_g
    hidden = (activated * up_pre).astype(BF16)
    expert_out = dot(hidden, down_mat, 1, 0).astype(BF16)
    returned = exchange(
        after(expert_out, out_grads).reshape(n_experts, capacity, width)
    ).reshape(slots, width)

    def summed(term):
        return lax.psum_scatter(term.astype(BF16), "rep", scatter_dimension=0, tiled=True)

    grad_down = summed(dot(hidden, out_grads, 0, 0))

    hidden_grad = dot(out_grads, down_mat, 1, 1)
    gate_delta = (
        hidden_grad * up_pre * sigmoid_g * (1.0 + gate_pre * (1.0 - sigmoid_g))
    ).astype(BF16)
    up_delta = (hidden_grad * activated).astype(BF16)
    grad_gate = summed(dot(rows_in, gate_delta, 0, 0))
    grad_up = summed(dot(rows_in, up_delta, 0, 0))
    row_grads = (dot(gate_delta, gate_mat, 1, 1) + dot(up_delta, up_mat, 1, 1)).astype(BF16)
    back_rows = exchange(row_grads.reshape(n_experts, capacity, width)).reshape(slots, width)

    layer_out = 0.0
    dots = []
    for k in range(top_count):
        pair_out = dot(picks[k], returned, 1, 0)
        layer_out = layer_out + weights[:, k][:, None] * pair_out
        dots.append(jnp.sum(pair_out * cotangent.astype(F32), axis=1))
    gate_grads = jnp.stack(dots, axis=1).astype(BF16)
    input_grads = dot(pick, back_rows, 1, 0).astype(BF16)
    return (
        layer_out.astype(BF16),
        input_grads,
        gate_grads,
        grad_gate.astype(F32)[None],
        grad_up.astype(F32)[None],
        grad_down.astype(F32)[None],
    )


def solution(mesh):
    tok = P(("rep", "ep"), None)
    mat = P("ep", None, None)
    grad = P("ep", "rep", None)
    return jax.shard_map(
        body,
        mesh=mesh,
        in_specs=(tok, tok, tok, mat, mat, mat, tok),
        out_specs=(tok, tok, tok, grad, grad, grad),
        check_vma=False,
    )
```

```python
import jax
import jax.numpy as jnp
from jax import lax
from jax.sharding import PartitionSpec as P

F32 = jnp.float32
BF16 = jnp.bfloat16


def dot(lhs, rhs, lhs_dim, rhs_dim):
    contract = (((lhs_dim,), (rhs_dim,)), ((), ()))
    return lax.dot_general(lhs, rhs, contract, preferred_element_type=F32)


def exchange(rows):
    return lax.all_to_all(rows, "ep", split_axis=0, concat_axis=0, tiled=True)


def after(value, *others):
    return lax.optimization_barrier((value, *others))[0]


def masks_of(n_rep):
    masks = []
    while 1 << len(masks) < n_rep:
        masks.append(1 << len(masks))
    return masks


def ranked(left):
    n_rep = lax.axis_size("rep")
    me = lax.axis_index("rep")
    block = left.shape[1] // n_rep
    return [
        lax.dynamic_slice_in_dim(left, (me ^ j) * block, block, axis=1) for j in range(n_rep)
    ]


def halved(blocks, right, order):
    n_rep = lax.axis_size("rep")
    rows = blocks[0].shape[1]

    def swap(part, mask):
        return lax.ppermute(part, "rep", [(i, i ^ mask) for i in range(n_rep)])

    live = [0]
    for mask in reversed(order):
        live = live + [j | mask for j in live]
    half = n_rep // 2
    product = lambda js: dot(jnp.concatenate([blocks[j] for j in js], axis=1), right, 0, 0)
    sent = swap(product(live[half:]).astype(BF16), order[0])
    total = product(live[:half]) + sent.astype(F32)
    for mask in order[1:]:
        half //= 2
        total = total.astype(BF16)
        sent = swap(total[half * rows :], mask)
        total = total[: half * rows].astype(F32) + sent.astype(F32)
    return total


def reduced(blocks, right):
    masks = masks_of(len(blocks))
    cut = (blocks[0].shape[1] // 2 + 15) // 16 * 16
    first = halved([b[:, :cut] for b in blocks], right, masks)
    second = halved([b[:, cut:] for b in blocks], right, masks[:1] + masks[:0:-1])
    return jnp.concatenate([first, second], axis=0)


def body(tokens, experts, gates, w_gate, w_up, w_down, cotangent):
    tok_rows, width = tokens.shape
    top_count = experts.shape[1]
    n_experts = lax.axis_size("ep")
    capacity = 3 * tok_rows * top_count // (2 * n_experts)
    slots = n_experts * capacity
    gate_mat, up_mat, down_mat = (w_gate[0], w_up[0], w_down[0])

    ids = jnp.arange(n_experts, dtype=jnp.int32)
    named = (experts[:, :, None] == ids).astype(BF16)
    visits = jnp.sum(named, axis=1)
    rows = jnp.arange(tok_rows, dtype=jnp.int32)
    earlier = (rows[:, None] > rows[None, :]).astype(BF16)
    rank = dot(earlier, visits, 1, 0)
    place = rank + (ids * capacity).astype(F32)[None, :]
    slot = jnp.sum(named.astype(F32) * place[:, None, :], axis=2).astype(jnp.int32)
    hit = [
        slot[:, k][:, None] == jnp.arange(slots, dtype=jnp.int32)[None, :]
        for k in range(top_count)
    ]
    picks = [h.astype(BF16) for h in hit]
    pick = sum(picks[1:], picks[0])
    weights = gates.astype(F32)

    dispatch = dot(pick, tokens, 0, 0).astype(BF16)
    rows_in = exchange(dispatch.reshape(n_experts, capacity, width)).reshape(slots, width)

    slot_gate = sum(
        jnp.sum(h.astype(F32) * weights[:, k][:, None], axis=0) for k, h in enumerate(hit)
    )
    grad_disp = (dot(pick, cotangent, 0, 0) * slot_gate[:, None]).astype(BF16)
    out_grads = exchange(
        after(grad_disp, rows_in).reshape(n_experts, capacity, width)
    ).reshape(slots, width)

    rows_ranked = ranked(rows_in)
    gate_pre = dot(rows_in, gate_mat, 1, 0)
    up_pre = dot(rows_in, up_mat, 1, 0)
    sigmoid_g = jax.nn.sigmoid(gate_pre)
    activated = gate_pre * sigmoid_g
    hidden = (activated * up_pre).astype(BF16)
    expert_out = dot(hidden, down_mat, 1, 0).astype(BF16)
    returned = exchange(
        after(expert_out, out_grads).reshape(n_experts, capacity, width)
    ).reshape(slots, width)

    grad_down = reduced(ranked(hidden), out_grads)

    hidden_grad = dot(out_grads, down_mat, 1, 1)
    gate_delta = (
        hidden_grad * up_pre * sigmoid_g * (1.0 + gate_pre * (1.0 - sigmoid_g))
    ).astype(BF16)
    up_delta = (hidden_grad * activated).astype(BF16)
    grad_gate = reduced(rows_ranked, gate_delta)
    grad_up = reduced(rows_ranked, up_delta)
    row_grads = (dot(gate_delta, gate_mat, 1, 1) + dot(up_delta, up_mat, 1, 1)).astype(BF16)
    back_rows = exchange(row_grads.reshape(n_experts, capacity, width)).reshape(slots, width)

    layer_out = 0.0
    dots = []
    for k in range(top_count):
        pair_out = dot(picks[k], returned, 1, 0)
        layer_out = layer_out + weights[:, k][:, None] * pair_out
        dots.append(jnp.sum(pair_out * cotangent.astype(F32), axis=1))
    gate_grads = jnp.stack(dots, axis=1).astype(BF16)
    input_grads = dot(pick, back_rows, 1, 0).astype(BF16)
    return (
        layer_out.astype(BF16),
        input_grads,
        gate_grads,
        grad_gate.astype(F32)[None],
        grad_up.astype(F32)[None],
        grad_down.astype(F32)[None],
    )


def solution(mesh):
    tok = P(("rep", "ep"), None)
    mat = P("ep", None, None)
    grad = P("ep", "rep", None)
    return jax.shard_map(
        body,
        mesh=mesh,
        in_specs=(tok, tok, tok, mat, mat, mat, tok),
        out_specs=(tok, tok, tok, grad, grad, grad),
        check_vma=False,
    )
```

```python
import jax
import jax.numpy as jnp
from jax import lax
from jax.sharding import PartitionSpec as P

F32 = jnp.float32
BF16 = jnp.bfloat16


def dot(lhs, rhs, lhs_dim, rhs_dim):
    contract = (((lhs_dim,), (rhs_dim,)), ((), ()))
    return lax.dot_general(lhs, rhs, contract, preferred_element_type=F32)


def exchange(rows):
    return lax.all_to_all(rows, "ep", split_axis=0, concat_axis=0, tiled=True)


def after(value, *others):
    return lax.optimization_barrier((value, *others))[0]


def masks_of(n_rep):
    masks = []
    while 1 << len(masks) < n_rep:
        masks.append(1 << len(masks))
    return masks


def ranked(left):
    n_rep = lax.axis_size("rep")
    me = lax.axis_index("rep")
    block = left.shape[1] // n_rep
    return [
        lax.dynamic_slice_in_dim(left, (me ^ j) * block, block, axis=1) for j in range(n_rep)
    ]


class Halving:
    def __init__(self, blocks, right, order):
        self.blocks, self.right, self.order = blocks, right, order
        self.live = [0]
        for mask in reversed(order):
            self.live = self.live + [j | mask for j in self.live]
        self.received = []

    def total(self, low, high):
        left = jnp.concatenate([self.blocks[j] for j in self.live[low:high]], axis=1)
        rows = self.blocks[0].shape[1]
        value = dot(left, self.right, 0, 0)
        for got in self.received:
            value = value + got[low * rows : high * rows].astype(F32)
        return value

    def send(self):
        stage = len(self.received)
        n_rep = len(self.live)
        high = n_rep >> stage
        part = self.total(high // 2, high).astype(BF16)
        mask = self.order[stage]
        self.received.append(lax.ppermute(part, "rep", [(i, i ^ mask) for i in range(n_rep)]))
        return part


def pieces(blocks, right):
    masks = masks_of(len(blocks))
    cut = (blocks[0].shape[1] // 2 + 15) // 16 * 16
    return [
        Halving([b[:, :cut] for b in blocks], right, masks),
        Halving([b[:, cut:] for b in blocks], right, masks[:1] + masks[:0:-1]),
    ]


def body(tokens, experts, gates, w_gate, w_up, w_down, cotangent):
    tok_rows, width = tokens.shape
    top_count = experts.shape[1]
    n_experts = lax.axis_size("ep")
    capacity = 3 * tok_rows * top_count // (2 * n_experts)
    slots = n_experts * capacity
    gate_mat, up_mat, down_mat = (w_gate[0], w_up[0], w_down[0])

    ids = jnp.arange(n_experts, dtype=jnp.int32)
    named = (experts[:, :, None] == ids).astype(BF16)
    visits = jnp.sum(named, axis=1)
    rows = jnp.arange(tok_rows, dtype=jnp.int32)
    earlier = (rows[:, None] > rows[None, :]).astype(BF16)
    rank = dot(earlier, visits, 1, 0)
    place = rank + (ids * capacity).astype(F32)[None, :]
    slot = jnp.sum(named.astype(F32) * place[:, None, :], axis=2).astype(jnp.int32)
    hit = [
        slot[:, k][:, None] == jnp.arange(slots, dtype=jnp.int32)[None, :]
        for k in range(top_count)
    ]
    picks = [h.astype(BF16) for h in hit]
    pick = sum(picks[1:], picks[0])
    weights = gates.astype(F32)

    dispatch = dot(pick, tokens, 0, 0).astype(BF16)
    rows_in = exchange(dispatch.reshape(n_experts, capacity, width)).reshape(slots, width)

    slot_gate = sum(
        jnp.sum(h.astype(F32) * weights[:, k][:, None], axis=0) for k, h in enumerate(hit)
    )
    grad_disp = (dot(pick, cotangent, 0, 0) * slot_gate[:, None]).astype(BF16)
    out_grads = exchange(
        after(grad_disp, rows_in).reshape(n_experts, capacity, width)
    ).reshape(slots, width)

    rows_ranked = ranked(rows_in)
    gate_pre = dot(rows_in, gate_mat, 1, 0)
    up_pre = dot(rows_in, up_mat, 1, 0)
    sigmoid_g = jax.nn.sigmoid(gate_pre)
    activated = gate_pre * sigmoid_g
    slope = up_pre * sigmoid_g * (1.0 + gate_pre * (1.0 - sigmoid_g))
    hidden = (activated * up_pre).astype(BF16)
    hidden, activated, slope = lax.optimization_barrier((hidden, activated, slope))
    expert_out = dot(hidden, down_mat, 1, 0).astype(BF16)
    hidden_ranked = ranked(hidden)
    out_grads, expert_out, *hidden_ranked = lax.optimization_barrier(
        (out_grads, expert_out, *hidden_ranked)
    )
    returned = exchange(expert_out.reshape(n_experts, capacity, width)).reshape(slots, width)

    down = pieces(hidden_ranked, out_grads)
    parts = [piece.send() for piece in down]
    hidden_grad = dot(after(out_grads, *parts), down_mat, 1, 1)
    gate_delta = (hidden_grad * slope).astype(BF16)
    up_delta = (hidden_grad * activated).astype(BF16)
    gate = pieces(rows_ranked, gate_delta)
    up = pieces(rows_ranked, up_delta)
    every = down + gate + up
    parts = [piece.send() for piece in gate + up]
    parts += [piece.send() for piece in down]
    gate_delta, up_delta = lax.optimization_barrier((gate_delta, up_delta, *parts))[:2]
    row_grads = (dot(gate_delta, gate_mat, 1, 1) + dot(up_delta, up_mat, 1, 1)).astype(BF16)
    for piece in gate + up:
        piece.send()
    row_grads, returned, *stage = lax.optimization_barrier(
        (row_grads, returned, *[piece.received[-1] for piece in every])
    )
    for piece, got in zip(every, stage):
        piece.received[-1] = got
    back_rows = exchange(row_grads.reshape(n_experts, capacity, width)).reshape(slots, width)
    for piece in every:
        while len(piece.received) < len(piece.order):
            piece.send()
    grad_gate, grad_up, grad_down = (
        jnp.concatenate([piece.total(0, 1) for piece in pair], axis=0)
        for pair in (gate, up, down)
    )

    layer_out = 0.0
    dots = []
    for k in range(top_count):
        pair_out = dot(picks[k], returned, 1, 0)
        layer_out = layer_out + weights[:, k][:, None] * pair_out
        dots.append(jnp.sum(pair_out * cotangent.astype(F32), axis=1))
    gate_grads = jnp.stack(dots, axis=1).astype(BF16)
    input_grads = dot(pick, back_rows, 1, 0).astype(BF16)
    return (
        layer_out.astype(BF16),
        input_grads,
        gate_grads,
        grad_gate.astype(F32)[None],
        grad_up.astype(F32)[None],
        grad_down.astype(F32)[None],
    )


def solution(mesh):
    tok = P(("rep", "ep"), None)
    mat = P("ep", None, None)
    grad = P("ep", "rep", None)
    return jax.shard_map(
        body,
        mesh=mesh,
        in_specs=(tok, tok, tok, mat, mat, mat, tok),
        out_specs=(tok, tok, tok, grad, grad, grad),
        check_vma=False,
    )
```

```python
import jax
import jax.numpy as jnp
from jax import lax
from jax.sharding import PartitionSpec as P

F32 = jnp.float32
BF16 = jnp.bfloat16


def dot(lhs, rhs, lhs_dim, rhs_dim):
    contract = (((lhs_dim,), (rhs_dim,)), ((), ()))
    return lax.dot_general(lhs, rhs, contract, preferred_element_type=F32)


def exchange(rows):
    return lax.all_to_all(rows, "ep", split_axis=0, concat_axis=0, tiled=True)


def after(value, *others):
    return lax.optimization_barrier((value, *others))[0]


def masks_of(n_rep):
    masks = []
    while 1 << len(masks) < n_rep:
        masks.append(1 << len(masks))
    return masks


def ranked(left):
    n_rep = lax.axis_size("rep")
    me = lax.axis_index("rep")
    block = left.shape[1] // n_rep
    cut = (block // 2 + 15) // 16 * 16
    return [
        [
            lax.dynamic_slice_in_dim(left, (me ^ j) * block + low, high - low, axis=1)
            for j in range(n_rep)
        ]
        for low, high in ((0, cut), (cut, block))
    ]


class Halving:
    def __init__(self, blocks, right, order):
        self.blocks, self.right, self.order = blocks, right, order
        self.live = [0]
        for mask in reversed(order):
            self.live = self.live + [j | mask for j in self.live]
        self.received = []

    def total(self, low, high):
        left = jnp.concatenate([self.blocks[j] for j in self.live[low:high]], axis=1)
        rows = self.blocks[0].shape[1]
        value = dot(left, self.right, 0, 0)
        for got in self.received:
            value = value + got[low * rows : high * rows].astype(F32)
        return value

    def send(self):
        stage = len(self.received)
        n_rep = len(self.live)
        high = n_rep >> stage
        part = self.total(high // 2, high).astype(BF16)
        mask = self.order[stage]
        self.received.append(lax.ppermute(part, "rep", [(i, i ^ mask) for i in range(n_rep)]))
        return part


def pieces(ranks, right):
    masks = masks_of(len(ranks[0]))
    orders = (masks, masks[:1] + masks[:0:-1])
    return [Halving(blocks, right, order) for blocks, order in zip(ranks, orders)]


def body(tokens, experts, gates, w_gate, w_up, w_down, cotangent):
    tok_rows, width = tokens.shape
    top_count = experts.shape[1]
    n_experts = lax.axis_size("ep")
    capacity = 3 * tok_rows * top_count // (2 * n_experts)
    slots = n_experts * capacity
    gate_mat, up_mat, down_mat = (w_gate[0], w_up[0], w_down[0])

    ids = jnp.arange(n_experts, dtype=jnp.int32)
    named = (experts[:, :, None] == ids).astype(BF16)
    visits = jnp.sum(named, axis=1)
    rows = jnp.arange(tok_rows, dtype=jnp.int32)
    earlier = (rows[:, None] > rows[None, :]).astype(BF16)
    rank = dot(earlier, visits, 1, 0)
    place = rank + (ids * capacity).astype(F32)[None, :]
    slot = jnp.sum(named.astype(F32) * place[:, None, :], axis=2).astype(jnp.int32)
    hit = [
        slot[:, k][:, None] == jnp.arange(slots, dtype=jnp.int32)[None, :]
        for k in range(top_count)
    ]
    picks = [h.astype(BF16) for h in hit]
    pick = sum(picks[1:], picks[0])
    weights = gates.astype(F32)

    dispatch = dot(pick, tokens, 0, 0).astype(BF16)
    rows_in = exchange(dispatch.reshape(n_experts, capacity, width)).reshape(slots, width)

    slot_gate = sum(
        jnp.sum(h.astype(F32) * weights[:, k][:, None], axis=0) for k, h in enumerate(hit)
    )
    grad_disp = (dot(pick, cotangent, 0, 0) * slot_gate[:, None]).astype(BF16)
    out_grads = exchange(
        after(grad_disp, rows_in).reshape(n_experts, capacity, width)
    ).reshape(slots, width)

    rows_ranked = ranked(rows_in)
    gate_pre = dot(rows_in, gate_mat, 1, 0)
    up_pre = dot(rows_in, up_mat, 1, 0)
    sigmoid_g = jax.nn.sigmoid(gate_pre)
    activated = gate_pre * sigmoid_g
    slope = up_pre * sigmoid_g * (1.0 + gate_pre * (1.0 - sigmoid_g))
    hidden = (activated * up_pre).astype(BF16)
    hidden, activated, slope = lax.optimization_barrier((hidden, activated, slope))
    expert_out = dot(hidden, down_mat, 1, 0).astype(BF16)
    hidden_ranked = ranked(hidden)
    out_grads, expert_out = lax.optimization_barrier((out_grads, expert_out))
    half = width // 2
    early = exchange(expert_out[:, :half].reshape(n_experts, capacity, half)).reshape(slots, half)
    late = exchange(
        after(expert_out[:, half:], early).reshape(n_experts, capacity, half)
    ).reshape(slots, half)

    down = pieces(hidden_ranked, out_grads)
    parts = [piece.send() for piece in down]
    hidden_grad = dot(after(out_grads, *parts), down_mat, 1, 1)
    gate_delta = (hidden_grad * slope).astype(BF16)
    up_delta = (hidden_grad * activated).astype(BF16)
    gate = pieces(rows_ranked, gate_delta)
    up = pieces(rows_ranked, up_delta)
    every = down + gate + up
    parts = [piece.send() for piece in gate + up]
    gate_delta, up_delta, early = lax.optimization_barrier((gate_delta, up_delta, early, *parts))[:3]
    row_grads = (dot(gate_delta, gate_mat, 1, 1) + dot(up_delta, up_mat, 1, 1)).astype(BF16)
    for piece in down + gate:
        piece.send()
    row_grads, late, *stage = lax.optimization_barrier(
        (row_grads, late, *[piece.received[0] for piece in up])
    )
    for piece, got in zip(up, stage):
        piece.received[0] = got
    returned = jnp.concatenate([early, late], axis=1)
    back_rows = exchange(row_grads.reshape(n_experts, capacity, width)).reshape(slots, width)
    for piece in every:
        while len(piece.received) < len(piece.order):
            piece.send()
        piece.blocks[0] = after(piece.blocks[0], piece.received[-2])
    grad_gate, grad_up, grad_down = (
        jnp.concatenate([piece.total(0, 1) for piece in pair], axis=0)
        for pair in (gate, up, down)
    )

    layer_out = 0.0
    dots = []
    for k in range(top_count):
        pair_out = dot(picks[k], returned, 1, 0)
        layer_out = layer_out + weights[:, k][:, None] * pair_out
        dots.append(jnp.sum(pair_out * cotangent.astype(F32), axis=1))
    gate_grads = jnp.stack(dots, axis=1).astype(BF16)
    input_grads = dot(pick, back_rows, 1, 0).astype(BF16)
    return (
        layer_out.astype(BF16),
        input_grads,
        gate_grads,
        grad_gate.astype(F32)[None],
        grad_up.astype(F32)[None],
        grad_down.astype(F32)[None],
    )


def solution(mesh):
    tok = P(("rep", "ep"), None)
    mat = P("ep", None, None)
    grad = P("ep", "rep", None)
    return jax.shard_map(
        body,
        mesh=mesh,
        in_specs=(tok, tok, tok, mat, mat, mat, tok),
        out_specs=(tok, tok, tok, grad, grad, grad),
        check_vma=False,
    )
```
